32 devices in a mesh: row: 4 (over y, core), col: 8 (over z, x).
Axes of the slice: x: 2, y: 2, z: 4, core: 2. Of those that a mesh axis runs over, the one named last changes fastest.
Arguments:
- weight: bfloat16 [8192, 26624], P('row', 'col'), may hold values from -0.59765625 to 0.59765625
- momentum: bfloat16 [8192, 26624], P('row', 'col'), may hold values from -6 to 6
- grad: bfloat16 [8192, 26624], P('row', 'col'), may hold values from -52 to 52
- right_factor: float32 [26624, 512], P('col'), may hold values from -6 to 6
Outputs:
- weight_next: bfloat16 [8192, 26624], P('row', 'col')
- momentum_next: bfloat16 [8192, 26624], P('row', 'col')
- right_next: float32 [26624, 512], P('col')
The draws below stay inside these ranges and needn't reach their ends.
All inputs are finite; a program needn't handle non-finite values.
Results may differ from the reference program's by a relative error of at most 0.009.
Values may be sent and summed in bfloat16 or wider, within the bound.
No kernel may reach another device: no remote copies, remote signals or barrier semaphores. Data moves between devices by JAX's collectives and lax.ppermute only.
A program may use at most 256 MiB of HBM per device.

```python
import math
import jax
import jax.numpy as jnp
from jax import lax

D = 8192
FF = 26624
RANK = 512


reach_terms = 48


carry_rate = 0.8


fresh_part = 0.6


def draw_grad(key, part):
    key = jax.random.fold_in(key, 7)
    key_rows, key_cols, key_base, key_phase, key_sign, key_line = jax.random.split(key, 6)
    top = math.log(3.2)
    rise = math.log(2.4)
    row_scale = jnp.exp(jax.random.uniform(key_rows, (D, 1), jnp.float32, 0.0, top))
    position = jnp.arange(FF, dtype=jnp.float32).reshape(1, FF) / jnp.float32(FF)
    col_rough = jax.random.uniform(key_cols, (1, FF), jnp.float32, 0.0, top - rise)
    col_scale = jnp.exp(rise * position + col_rough)
    phase = jax.random.randint(key_phase, (), 0, 4)
    columns = jnp.arange(FF, dtype=jnp.int32).reshape(1, FF)
    period_scale = jnp.where(columns % 4 == phase, jnp.float32(2.0), jnp.float32(0.7))
    signs = jnp.where(jax.random.bernoulli(key_sign, 0.5, (D, 1)), jnp.float32(1.0), jnp.float32(-1.0))
    line = jnp.clip(jax.random.normal(key_line, (1, FF), jnp.float32), -4.0, 4.0)
    common = 1.5 * signs * line
    base = jnp.clip(jax.random.normal(key_base, (D, FF), jnp.float32), -5.0, 5.0)
    total = base * row_scale * col_scale * period_scale + common
    return jnp.clip(total, -52.0, 52.0).astype(jnp.bfloat16)


def draw_right_factor(key, part):
    key = jax.random.fold_in(key, 11)
    width = RANK + reach_terms - 1
    noise = jnp.clip(jax.random.normal(key, (FF, width), jnp.float32), -5.0, 5.0)
    total = jnp.zeros((FF, RANK), jnp.float32)
    for step in range(reach_terms):
        start = reach_terms - 1 - step
        total = total + jnp.float32(fresh_part * carry_rate ** step) * noise[:, start:start + RANK]
    return jnp.clip(total, -6.0, 6.0).astype(jnp.float32)


def levels(own_key, shape, cuts, low, largest):
    def one(dim, blocks):
        steps = jax.random.uniform(jax.random.fold_in(jax.random.fold_in(own_key, 6), dim), (blocks,), jnp.float32, low / len(cuts), largest / len(cuts))
        return jnp.repeat(jnp.exp(steps), shape[dim] // blocks).reshape((-1,) + (1,) * (len(shape) - dim - 1))

    loudness = one(*cuts[0])
    for cut in cuts[1:]:
        loudness = loudness * one(*cut)
    return loudness


def scatter_about(rng, extent, scale, reach, pieces=(), kind=jnp.bfloat16):
    level = levels(rng, extent, pieces, -0.22, 0.18) if pieces else 1.0
    drawn = jax.random.normal(rng, extent, jnp.float32) * scale * level
    return jnp.minimum(jnp.maximum(drawn, -reach), reach).astype(kind)


def setup_inputs(seed: int = 0) -> dict:
    key_of = jax.random.split(jax.random.key(seed), 5)
    weight = scatter_about(key_of[0], (D, FF), 0.1, 0.59765625, ((0, 4), (1, 8)))
    momentum = scatter_about(key_of[1], (D, FF), 1.0, 6.0, ((0, 4), (1, 8)))
    grad = draw_grad(jax.random.fold_in(key_of[4], 71), 0)
    right_factor = draw_right_factor(jax.random.fold_in(key_of[4], 71), 0)
    return dict(weight=weight, momentum=momentum, grad=grad, right_factor=right_factor)


FEEDBACK_CUT = 0.25
STEP_SIZE = 0.1
EPSILON_SQ = 1e-06

def orthonormal(left_prod, gram_mat):
    factor_low = jnp.linalg.cholesky(gram_mat)
    return lax.linalg.triangular_solve(factor_low, left_prod, left_side=False, lower=True, transpose_a=True)

def reference(weight, momentum, grad, right_factor):
    buffer = (momentum.astype(jnp.float32) + grad.astype(jnp.float32)).astype(jnp.bfloat16)
    right_in = right_factor.astype(jnp.bfloat16)
    left_prod = jnp.dot(buffer.astype(jnp.float32), right_in.astype(jnp.float32), preferred_element_type=jnp.float32)
    gram_mat = jnp.dot(left_prod.T.astype(jnp.float32), left_prod.astype(jnp.float32), precision=lax.Precision.HIGHEST, preferred_element_type=jnp.float32)
    ortho_rows = orthonormal(left_prod, gram_mat).astype(jnp.bfloat16)
    back_prod = jnp.dot(buffer.T.astype(jnp.float32), ortho_rows.astype(jnp.float32), preferred_element_type=jnp.float32)
    squares = lax.optimization_barrier(jnp.sum(back_prod * back_prod, axis=0))
    right_next = back_prod * (jnp.sqrt(jnp.float32(FF)) / jnp.sqrt(squares + EPSILON_SQ))
    back_half = back_prod.astype(jnp.bfloat16)
    right_half = right_next.astype(jnp.bfloat16)
    momentum_next = (buffer.astype(jnp.float32) - FEEDBACK_CUT * jnp.dot(ortho_rows.astype(jnp.float32), back_half.T.astype(jnp.float32), preferred_element_type=jnp.float32)).astype(jnp.bfloat16)
    weight_next = (weight.astype(jnp.float32) - STEP_SIZE * jnp.dot(ortho_rows.astype(jnp.float32), right_half.T.astype(jnp.float32), preferred_element_type=jnp.float32)).astype(jnp.bfloat16)
    return (weight_next, momentum_next, right_next)
```

```python
import jax
import jax.numpy as jnp
from jax import lax
from jax.experimental import pallas as pl
from jax.experimental.pallas import tpu as pltpu
from jax.sharding import PartitionSpec as P

FEEDBACK_CUT = 0.25
STEP_SIZE = 0.1
EPSILON_SQ = 1e-06
PANEL = 32
LANES = 128

f32 = jnp.float32
bf16 = jnp.bfloat16


def split3(value):
    one = value.astype(bf16)
    rest = value - one.astype(f32)
    two = rest.astype(bf16)
    three = (rest - two.astype(f32)).astype(bf16)
    return one, two, three


def inverse_factor_kernel(gram_ref, one_ref, two_ref, work):
    size = gram_ref.shape[0]
    tiles = size // LANES
    work[...] = gram_ref[...]

    @pl.loop(0, size // PANEL)
    def _(panel):
        top = pl.multiple_of(panel * PANEL, PANEL)
        tile = pl.multiple_of((top // LANES) * LANES, LANES)
        rows = work[pl.ds(top, PANEL), :]
        diag = pltpu.roll(
            work[pl.ds(top, PANEL), pl.ds(tile, LANES)], lax.rem(LANES - (top - tile), LANES), 1
        )
        lane = lax.broadcasted_iota(jnp.int32, (PANEL, size), 1)
        row = lax.broadcasted_iota(jnp.int32, (PANEL, size), 0)
        inside = (lane >= top) & (lane < top + PANEL)
        rows = jnp.where(inside, jnp.where(lane - top == row, 1.0, 0.0).astype(f32), rows)
        sub = lax.broadcasted_iota(jnp.int32, (PANEL, LANES), 0)
        cols = [
            jnp.broadcast_to(diag[k // 8 * 8 :, k : k + 1], (PANEL - k // 8 * 8, LANES))
            for k in range(PANEL)
        ]
        pivots = jnp.zeros((PANEL, LANES), f32)
        for j in range(PANEL):
            low = j // 8 * 8
            col = cols[j]
            pivot = col[j - low : j - low + 1, :]
            pivots = jnp.where(sub == j, pivot, pivots)
            if j == PANEL - 1:
                break
            factor = jnp.where(sub[low:] > j, col * (1.0 / pivot), 0.0)
            for k in range(j + 1, PANEL):
                cols[k] = cols[k] - col[k // 8 * 8 - low :, :] * factor[k - low : k - low + 1, :]
            step = jnp.concatenate([factor] * tiles, axis=1) * rows[j : j + 1, :]
            rows = jnp.concatenate([rows[:low], rows[low:] - step], axis=0) if low else rows - step
        scale = lax.rsqrt(pivots)
        scale = scale * (1.5 - 0.5 * pivots * scale * scale)
        rows = rows * jnp.concatenate([scale] * tiles, axis=1)
        work[pl.ds(top, PANEL), :] = rows
        b1, b2, b3 = split3(rows)
        a1, a2, a3 = split3(jnp.where(lane >= top + PANEL, rows, 0.0))
        lhs = jnp.concatenate([a1, a1, a2, a1, a2, a3], axis=0)
        rhs = jnp.concatenate([b1, b2, b1, b3, b2, b1], axis=0)
        for c in range(tiles):
            at = slice(c * LANES, (c + 1) * LANES)

            @pl.when((c + 1) * LANES > top + PANEL)
            def _():
                change = lax.dot_general(
                    lhs[:, at], rhs, (((0,), (0,)), ((), ())), preferred_element_type=f32
                )
                across = lax.broadcasted_iota(jnp.int32, (LANES, size), 1)
                down = lax.broadcasted_iota(jnp.int32, (LANES, size), 0) + c * LANES
                gone = (across >= top) & (across < top + PANEL) & (down >= top + PANEL)
                work[at, :] = jnp.where(gone, 0.0, work[at, :]) - change

    across = lax.broadcasted_iota(jnp.int32, (size, size), 1)
    down = lax.broadcasted_iota(jnp.int32, (size, size), 0)
    inverse = jnp.where(across <= down, work[...], 0.0)
    one = inverse.astype(bf16)
    one_ref[...] = one
    two_ref[...] = (inverse - one.astype(f32)).astype(bf16)


def inverse_factor(gram_mat):
    size = gram_mat.shape[0]
    return pl.pallas_call(
        inverse_factor_kernel,
        out_shape=[jax.ShapeDtypeStruct((size, size), bf16)] * 2,
        in_specs=[pl.BlockSpec(memory_space=pltpu.VMEM)],
        out_specs=[pl.BlockSpec(memory_space=pltpu.VMEM)] * 2,
        scratch_shapes=[pltpu.VMEM((size, size), f32)],
        compiler_params=pltpu.CompilerParams(vmem_limit_bytes=24 << 20),
        cost_estimate=pl.CostEstimate(flops=int(2e10), bytes_accessed=2 << 20, transcendentals=0),
        name="inverse_factor",
    )(gram_mat)


def swap(value, axis, count, bit):
    return lax.ppermute(value, axis, [(i, i ^ bit) for i in range(count)])


def take(value, part, parts):
    share = value.shape[0] // parts
    return lax.dynamic_slice_in_dim(value, part * share, share, 0)


def sum_share(value, axis, count):
    me = lax.axis_index(axis)
    bit = 1
    while bit < count:
        mine = (me // bit) % 2
        got = swap(take(value, 1 - mine, 2).astype(bf16), axis, count, bit)
        value = take(value, mine, 2) + got.astype(f32)
        bit *= 2
    return value


def join_shares(value, axis, count):
    me = lax.axis_index(axis)
    bit = count // 2
    while bit >= 1:
        got = swap(value, axis, count, bit)
        first = (me // bit) % 2 == 0
        value = jnp.concatenate([jnp.where(first, value, got), jnp.where(first, got, value)], axis=0)
        bit //= 2
    return value


def sum_all(value, axis, count, low=1):
    bit = low
    while bit < count:
        value = value + swap(value, axis, count, bit)
        bit *= 2
    return value


def make_on_device(n_row, n_col):
    def on_device(weight, momentum, grad, right_factor):
        full = right_factor.shape[0] * n_col
        core = lax.axis_index("row") % 2
        buffer = (momentum.astype(f32) + grad.astype(f32)).astype(bf16)
        right_in = right_factor.astype(bf16)
        left_part = jnp.dot(buffer, right_in, preferred_element_type=f32)
        left_share = sum_share(left_part, "col", n_col).astype(bf16)
        left_prod = join_shares(left_share, "col", n_col)

        gram_part = lax.dot_general(
            left_prod, left_prod, (((0,), (0,)), ((), ())), preferred_element_type=f32
        )
        gram_half = take(gram_part, core, 2) + swap(take(gram_part, 1 - core, 2), "row", n_row, 1)
        gram_half = sum_all(gram_half, "row", n_row, 2)
        gram_other = swap(gram_half, "row", n_row, 1)
        gram_mat = jnp.concatenate(
            [
                jnp.where(core == 0, gram_half, gram_other),
                jnp.where(core == 0, gram_other, gram_half),
            ],
            axis=0,
        )

        inv_one, inv_two = inverse_factor(gram_mat)
        ortho_rows = (
            lax.dot_general(left_prod, inv_one, (((1,), (1,)), ((), ())), preferred_element_type=f32)
            + lax.dot_general(left_prod, inv_two, (((1,), (1,)), ((), ())), preferred_element_type=f32)
        ).astype(bf16)

        back_part = lax.dot_general(
            buffer, ortho_rows, (((0,), (0,)), ((), ())), preferred_element_type=f32
        )
        sent = take(back_part, 1 - core, 2).astype(bf16)
        back_own = take(back_part, core, 2) + swap(sent, "row", n_row, 1).astype(f32)
        bit = 2
        while bit < n_row:
            sent = back_own.astype(bf16)
            back_own = sent.astype(f32) + swap(sent, "row", n_row, bit).astype(f32)
            bit *= 2
        squares = jnp.sum(back_own * back_own, axis=0, keepdims=True)
        back_own = back_own.astype(bf16)
        back_other = swap(back_own, "row", n_row, 1)
        back_half = jnp.concatenate(
            [
                jnp.where(core == 0, back_own, back_other),
                jnp.where(core == 0, back_other, back_own),
            ],
            axis=0,
        )
        squares = squares + swap(squares, "row", n_row, 1)
        squares = sum_all(squares, "col", n_col)
        scale = jnp.sqrt(f32(full)) / jnp.sqrt(squares + EPSILON_SQ)

        feedback = jnp.einsum("ik,jk->ij", ortho_rows, back_half, preferred_element_type=f32)
        momentum_next = (buffer.astype(f32) - FEEDBACK_CUT * feedback).astype(bf16)
        right_next = back_half.astype(f32) * scale
        right_half = right_next.astype(bf16)
        update = jnp.einsum("ik,jk->ij", ortho_rows, right_half, preferred_element_type=f32)
        weight_next = (weight.astype(f32) - STEP_SIZE * update).astype(bf16)
        return (weight_next, momentum_next, right_next)

    return on_device


def solution(mesh):
    in_specs = (P("row", "col"), P("row", "col"), P("row", "col"), P("col", None))
    out_specs = (P("row", "col"), P("row", "col"), P("col", None))
    return jax.shard_map(
        make_on_device(mesh.shape["row"], mesh.shape["col"]),
        mesh=mesh,
        in_specs=in_specs,
        out_specs=out_specs,
        check_vma=False,
    )
```

```python
import functools

import jax
import jax.numpy as jnp
from jax import lax
from jax.experimental import pallas as pl
from jax.experimental.pallas import tpu as pltpu
from jax.sharding import PartitionSpec as P

FEEDBACK_CUT = 0.25
STEP_SIZE = 0.1
EPSILON_SQ = 1e-06
PANEL = 32
PIECES = 2
LANES = 128

f32 = jnp.float32
bf16 = jnp.bfloat16


def split3(value):
    one = value.astype(bf16)
    rest = value - one.astype(f32)
    two = rest.astype(bf16)
    three = (rest - two.astype(f32)).astype(bf16)
    return one, two, three


IN_VMEM = pl.BlockSpec(memory_space=pltpu.VMEM)
ANYWHERE = pl.BlockSpec(memory_space=pltpu.HBM)
BIG = pltpu.CompilerParams(vmem_limit_bytes=48 << 20)
SHORT = pl.CostEstimate(flops=1, bytes_accessed=1, transcendentals=0)


def eliminate(work, first):
    count, size = work.shape
    tiles = size // LANES

    @pl.loop(0, count // PANEL)
    def _(panel):
        top = pl.multiple_of(panel * PANEL, PANEL)
        left = pl.multiple_of(first + panel * PANEL, PANEL)
        tile = pl.multiple_of((left // LANES) * LANES, LANES)
        rows = work[pl.ds(top, PANEL), :]
        diag = pltpu.roll(
            work[pl.ds(top, PANEL), pl.ds(tile, LANES)], lax.rem(LANES - (left - tile), LANES), 1
        )
        lane = lax.broadcasted_iota(jnp.int32, (PANEL, size), 1)
        row = lax.broadcasted_iota(jnp.int32, (PANEL, size), 0)
        inside = (lane >= left) & (lane < left + PANEL)
        rows = jnp.where(inside, jnp.where(lane - left == row, 1.0, 0.0).astype(f32), rows)
        sub = lax.broadcasted_iota(jnp.int32, (PANEL, LANES), 0)
        cols = [
            jnp.broadcast_to(diag[k // 8 * 8 :, k : k + 1], (PANEL - k // 8 * 8, LANES))
            for k in range(PANEL)
        ]
        pivots = jnp.zeros((PANEL, LANES), f32)
        for j in range(PANEL):
            low = j // 8 * 8
            col = cols[j]
            pivot = col[j - low : j - low + 1, :]
            pivots = jnp.where(sub == j, pivot, pivots)
            if j == PANEL - 1:
                break
            factor = jnp.where(sub[low:] > j, col * (1.0 / pivot), 0.0)
            for k in range(j + 1, PANEL):
                cols[k] = cols[k] - col[k // 8 * 8 - low :, :] * factor[k - low : k - low + 1, :]
            step = jnp.concatenate([factor] * tiles, axis=1) * rows[j : j + 1, :]
            rows = jnp.concatenate([rows[:low], rows[low:] - step], axis=0) if low else rows - step
        scale = lax.rsqrt(pivots)
        scale = scale * (1.5 - 0.5 * pivots * scale * scale)
        rows = rows * jnp.concatenate([scale] * tiles, axis=1)
        work[pl.ds(top, PANEL), :] = rows
        lhs = stack_left(jnp.where(lane >= left + PANEL, rows, 0.0)[:, first:], 0)
        rhs = stack_right(rows, 0)
        for c in range(count // LANES):
            at = slice(c * LANES, (c + 1) * LANES)

            @pl.when((c + 1) * LANES > top + PANEL)
            def _():
                change = lax.dot_general(
                    lhs[:, at], rhs, (((0,), (0,)), ((), ())), preferred_element_type=f32
                )
                across = lax.broadcasted_iota(jnp.int32, (LANES, size), 1)
                down = lax.broadcasted_iota(jnp.int32, (LANES, size), 0) + c * LANES
                gone = (across >= left) & (across < left + PANEL) & (down >= top + PANEL)
                work[at, :] = jnp.where(gone, 0.0, work[at, :]) - change


def stack_left(value, axis):
    one, two, three = split3(value)
    return jnp.concatenate([one, one, two, one, two, three], axis=axis)


def stack_right(value, axis):
    one, two, three = split3(value)
    return jnp.concatenate([one, two, one, three, two, one], axis=axis)


def store_inverse(work, first, out_ref, one_ref, two_ref):
    across = lax.broadcasted_iota(jnp.int32, work.shape, 1)
    down = lax.broadcasted_iota(jnp.int32, work.shape, 0) + first
    inverse = jnp.where(across <= down, work[...], 0.0)
    one = inverse.astype(bf16)
    one_ref[...] = one
    two_ref[...] = (inverse - one.astype(f32)).astype(bf16)
    if out_ref is not None:
        out_ref[...] = inverse


def first_inverse_kernel(gram_ref, out_ref, one_ref, two_ref, work):
    work[...] = gram_ref[...]
    eliminate(work, 0)
    store_inverse(work, 0, out_ref, one_ref, two_ref)


def second_inverse_kernel(gram_ref, inverse_ref, _, one_ref, two_ref, work):
    first = inverse_ref.shape[0]
    inverse = inverse_ref[...]
    across = (((1,), (1,)), ((), ()))
    plain = (((1,), (0,)), ((), ()))
    low = lax.dot_general(
        stack_left(gram_ref[:, :first], 1), stack_right(inverse, 1), across, preferred_element_type=f32
    )
    low_left = stack_left(low, 1)
    work[:, :first] = -lax.dot_general(
        low_left, stack_right(inverse, 0), plain, preferred_element_type=f32
    )
    work[:, first:] = gram_ref[:, first:] - lax.dot_general(
        low_left, stack_right(low, 1), across, preferred_element_type=f32
    )
    eliminate(work, first)
    store_inverse(work, first, None, one_ref, two_ref)


def first_inverse(gram_mat):
    size = gram_mat.shape[0]
    return pl.pallas_call(
        first_inverse_kernel,
        out_shape=[
            jax.ShapeDtypeStruct((size, size), f32),
            jax.ShapeDtypeStruct((size, size), bf16),
            jax.ShapeDtypeStruct((size, size), bf16),
        ],
        in_specs=[pl.BlockSpec(memory_space=pltpu.VMEM)],
        out_specs=[pl.BlockSpec(memory_space=pltpu.VMEM)] * 3,
        scratch_shapes=[pltpu.VMEM((size, size), f32)],
        compiler_params=pltpu.CompilerParams(vmem_limit_bytes=24 << 20),
        cost_estimate=SHORT,
        name="first_inverse",
    )(gram_mat)


def second_inverse(gram_rows, inverse, earlier):
    shape = gram_rows.shape
    return pl.pallas_call(
        second_inverse_kernel,
        out_shape=[jax.ShapeDtypeStruct(shape, bf16)] * 2,
        in_specs=[IN_VMEM, IN_VMEM, ANYWHERE],
        out_specs=[pl.BlockSpec(memory_space=pltpu.VMEM)] * 2,
        scratch_shapes=[pltpu.VMEM(shape, f32)],
        compiler_params=pltpu.CompilerParams(vmem_limit_bytes=24 << 20),
        cost_estimate=SHORT,
        name="second_inverse",
    )(gram_rows, inverse, earlier)


def chunks_of(columns):
    wide = 512 if columns % LANES == 0 else columns
    return [(at, min(wide, columns - at)) for at in range(0, columns, wide)]


def copies(source, target, semaphores):
    return [
        pltpu.make_async_copy(source.at[:, pl.ds(at, wide)], target.at[:, pl.ds(at, wide)], semaphores.at[i])
        for i, (at, wide) in enumerate(chunks_of(source.shape[1]))
    ]


def back_kernel(count, has_ortho, _, *refs):
    left_refs, refs = refs[:count], refs[count:]
    one_ref, two_ref, refs = refs[0], refs[1], refs[2:]
    if has_ortho:
        earlier_ref, refs = refs[0], refs[1:]
    buffer_ref, ortho_ref, back_ref, held, arrived = refs
    coming = copies(buffer_ref, held, arrived)
    for copy in coming:
        copy.start()
    total = None
    at = 0
    for left_ref in left_refs:
        wide = left_ref.shape[1]
        for part in (one_ref, two_ref):
            term = lax.dot_general(
                left_ref[...], part[:, at : at + wide], (((1,), (1,)), ((), ())), preferred_element_type=f32
            )
            total = term if total is None else total + term
        at += wide
    if has_ortho:
        ortho_ref[:, : earlier_ref.shape[1]] = earlier_ref[...]
        ortho_ref[:, earlier_ref.shape[1] :] = total.astype(bf16)
    else:
        ortho_ref[...] = total.astype(bf16)
    turned = total.T.astype(bf16)
    for copy, (at, wide) in zip(coming, chunks_of(held.shape[1])):
        copy.wait()
        back_ref[:, at : at + wide] = jnp.dot(
            turned, held[:, at : at + wide], preferred_element_type=f32
        ).astype(bf16)


def back_product(before, lefts, one, two, earlier, buffer):
    rows, columns = buffer.shape
    rank = one.shape[0]
    extra = [] if earlier is None else [earlier]
    all_rank = rank + sum(v.shape[1] for v in extra)
    return pl.pallas_call(
        functools.partial(back_kernel, len(lefts), bool(extra)),
        out_shape=[
            jax.ShapeDtypeStruct((rows, all_rank), bf16),
            jax.ShapeDtypeStruct((rank, columns), bf16),
        ],
        in_specs=[ANYWHERE] + [IN_VMEM] * (len(lefts) + 2 + len(extra)) + [ANYWHERE],
        out_specs=[IN_VMEM, IN_VMEM],
        scratch_shapes=[
            pltpu.VMEM((rows, columns), bf16),
            pltpu.SemaphoreType.DMA((len(chunks_of(columns)),)),
        ],
        compiler_params=BIG,
        cost_estimate=SHORT,
        name="back_product",
    )(before, *lefts, one, two, *extra, buffer)


def pick_kernel(which_ref, part_ref, _, out_ref):
    rows = out_ref.shape[0]
    out_ref[...] = part_ref[pl.ds(pl.multiple_of(which_ref[0] * rows, rows), rows), :]


def pick(part, which, earlier):
    return pl.pallas_call(
        pick_kernel,
        out_shape=jax.ShapeDtypeStruct((part.shape[0] // 2, part.shape[1]), part.dtype),
        in_specs=[pl.BlockSpec(memory_space=pltpu.SMEM), IN_VMEM, ANYWHERE],
        out_specs=IN_VMEM,
        compiler_params=pltpu.CompilerParams(vmem_limit_bytes=16 << 20),
        cost_estimate=SHORT,
        name="pick",
    )(which.reshape(1).astype(jnp.int32), part, earlier)


def update_kernel(cut, scaled, ortho_ref, *refs):
    back_refs, refs = refs[:PIECES], refs[PIECES:]
    if scaled:
        scale_refs, refs = refs[:PIECES], refs[PIECES:]
        value_ref, out_ref, right_ref, held, arrived, left, turned, turned_left = refs
    else:
        value_ref, out_ref, held, arrived, left = refs
    coming = copies(value_ref, held, arrived)
    going = copies(held, out_ref, left)
    for copy in coming:
        copy.start()
    rows, columns = held.shape
    tall = min(512, rows)
    leaving = []
    for i, (at, wide) in enumerate(chunks_of(columns)):
        backs = [ref[:, at : at + wide] for ref in back_refs]
        if scaled:
            rights = [v.astype(f32) * ref[...] for v, ref in zip(backs, scale_refs)]
            column = 0
            for v in rights:
                turned[at : at + wide, column : column + v.shape[0]] = v.T
                column += v.shape[0]
            copy = pltpu.make_async_copy(
                turned.at[pl.ds(at, wide), :], right_ref.at[pl.ds(at, wide), :], turned_left.at[i]
            )
            copy.start()
            leaving.append(copy)
            backs = [v.astype(bf16) for v in rights]
        back = jnp.concatenate(backs, axis=0)
        coming[i].wait()
        for top in range(0, rows, tall):
            here = (slice(top, top + tall), slice(at, at + wide))
            change = jnp.dot(ortho_ref[top : top + tall, :], back, preferred_element_type=f32)
            held[here] = (held[here].astype(f32) - cut * change).astype(bf16)
        going[i].start()
    for copy in going + leaving:
        copy.wait()


def update(cut, ortho, backs, scales, value, name):
    rows, columns = value.shape
    scaled = bool(scales)
    rank = sum(v.shape[0] for v in backs)
    count = len(chunks_of(columns))
    out_shape = [jax.ShapeDtypeStruct(value.shape, value.dtype)]
    scratch = [
        pltpu.VMEM((rows, columns), bf16),
        pltpu.SemaphoreType.DMA((count,)),
        pltpu.SemaphoreType.DMA((count,)),
    ]
    if scaled:
        out_shape.append(jax.ShapeDtypeStruct((columns, rank), f32))
        scratch += [pltpu.VMEM((columns, rank), f32), pltpu.SemaphoreType.DMA((count,))]
    return pl.pallas_call(
        functools.partial(update_kernel, cut, scaled),
        out_shape=out_shape,
        in_specs=[IN_VMEM] * (1 + len(backs) + len(scales)) + [ANYWHERE],
        out_specs=[ANYWHERE] * len(out_shape),
        scratch_shapes=scratch,
        compiler_params=BIG,
        cost_estimate=SHORT,
        name=name,
    )(ortho, *backs, *scales, value)


def swap(value, axis, count, bit):
    return lax.ppermute(value, axis, [(i, i ^ bit) for i in range(count)])


def take(value, part, parts):
    share = value.shape[0] // parts
    return lax.dynamic_slice_in_dim(value, part * share, share, 0)


def in_order(first, own, other):
    return jnp.concatenate([jnp.where(first, own, other), jnp.where(first, other, own)], axis=0)


def make_on_device(n_row, n_col):
    n_line = n_col // 2

    def along(value, steps):
        return lax.ppermute(
            value, "col", [(i, (i // 2 + steps) % n_line * 2 + i % 2) for i in range(n_col)]
        )

    def on_device(weight, momentum, grad, right_factor):
        full = right_factor.shape[0] * n_col
        core = lax.axis_index("row") % 2
        side = lax.axis_index("col") % 2
        place = lax.axis_index("col") // 2

        def reduce_pair(part):
            sent = take(part, 1 - side, 2).astype(bf16)
            return take(part, side, 2) + swap(sent, "col", n_col, 1).astype(f32)

        def reduce_line(part):
            total = take(part, place, n_line)
            for d in range(1, n_line):
                total = total + along(
                    take(part, (place + d) % n_line, n_line).astype(bf16), d
                ).astype(f32)
            return total.astype(bf16)

        def gather_line(share):
            rows = share.shape[0]
            joined = jnp.zeros((n_line * rows, share.shape[1]), bf16)
            joined = lax.dynamic_update_slice_in_dim(joined, share, place * rows, 0)
            for d in range(1, n_line):
                at = (place + n_line - d) % n_line * rows
                joined = lax.dynamic_update_slice_in_dim(joined, along(share, d), at, 0)
            return joined

        def gather_pair(half):
            return in_order(side == 0, half, swap(half, "col", n_col, 1))

        def sum_row(part):
            half = take(part, core, 2) + swap(take(part, 1 - core, 2), "row", n_row, 1)
            bit = 2
            while bit < n_row:
                half = half + swap(half, "row", n_row, bit)
                bit *= 2
            return half

        def join_cores(half):
            return in_order(core == 0, half, swap(half, "row", n_row, 1))

        def sum_core(part, sent):
            own = take(part, core, 2).astype(f32) + swap(sent, "row", n_row, 1).astype(f32)
            return own.astype(bf16)

        def sum_chips(own):
            bit = 2
            while bit < n_row:
                own = own.astype(f32) + swap(own, "row", n_row, bit).astype(f32)
                bit *= 2
                if bit < n_row:
                    own = own.astype(bf16)
            return own

        def squares_of(own):
            return jnp.sum(own * own, axis=1, keepdims=True).reshape(1, -1)

        def sum_squares(squares):
            squares = squares + swap(squares, "col", n_col, 1)
            others = [along(squares, d) for d in range(1, n_line)]
            for other in others:
                squares = squares + other
            return in_order(core == 0, squares, swap(squares, "row", n_row, 1))

        buffer = (momentum.astype(f32) + grad.astype(f32)).astype(bf16)
        right_in = right_factor.astype(bf16)
        piece = right_in.shape[1] // 2
        part_1 = jnp.dot(buffer, right_in[:, :piece], preferred_element_type=f32)
        part_2 = jnp.dot(buffer, right_in[:, piece:], preferred_element_type=f32)
        over_rows = (((0,), (0,)), ((), ()))

        pair_1 = reduce_pair(part_1)
        share_1 = reduce_line(pair_1)
        pair_2 = reduce_pair(part_2)
        line_1 = gather_line(share_1)
        share_2 = reduce_line(pair_2)
        left_1 = gather_pair(line_1)
        line_2 = gather_line(share_2)
        gram_1 = join_cores(
            sum_row(lax.dot_general(left_1, left_1, over_rows, preferred_element_type=f32))
        )
        left_2 = gather_pair(line_2)
        gram_2 = sum_row(
            jnp.concatenate(
                [
                    lax.dot_general(left_2, left_1, over_rows, preferred_element_type=f32),
                    lax.dot_general(left_2, left_2, over_rows, preferred_element_type=f32),
                ],
                axis=1,
            )
        )
        inverse_1, one_1, two_1 = first_inverse(gram_1)
        ortho_1, back_part_1 = back_product(gram_2, [left_1], one_1, two_1, None, buffer)
        core_1 = sum_core(back_part_1, take(back_part_1, 1 - core, 2))
        chips_1 = sum_chips(core_1)
        one_2, two_2 = second_inverse(join_cores(gram_2), inverse_1, core_1)
        ortho, back_part_2 = back_product(core_1, [left_1, left_2], one_2, two_2, ortho_1, buffer)
        core_2 = sum_core(back_part_2, pick(back_part_2, 1 - core, chips_1))
        chips_2 = sum_chips(core_2)
        back_1 = join_cores(chips_1.astype(bf16))
        back_2 = join_cores(chips_2.astype(bf16))
        squares_1, squares_2 = squares_of(chips_1), squares_of(chips_2)
        (momentum_next,) = update(FEEDBACK_CUT, ortho, [back_1, back_2], [], buffer, "momentum_update")
        squares = jnp.concatenate([squares_1, squares_2], axis=1).reshape(2, -1)
        squares = sum_squares(squares)
        squares = jnp.concatenate([squares[0:1], squares[2:3], squares[1:2], squares[3:4]], axis=0).reshape(2, piece, 1)
        scale = jnp.sqrt(f32(full)) / jnp.sqrt(squares + EPSILON_SQ)

        backs = [back_1, back_2]
        weight_next, right_next = update(
            STEP_SIZE, ortho, backs, [scale[0], scale[1]], weight, "weight_update"
        )
        return (weight_next, momentum_next, right_next)

    return on_device


def solution(mesh):
    in_specs = (P("row", "col"), P("row", "col"), P("row", "col"), P("col", None))
    out_specs = (P("row", "col"), P("row", "col"), P("col", None))
    return jax.shard_map(
        make_on_device(mesh.shape["row"], mesh.shape["col"]),
        mesh=mesh,
        in_specs=in_specs,
        out_specs=out_specs,
        check_vma=False,
    )
```

```python
import functools

import jax
import jax.numpy as jnp
from jax import lax
from jax.experimental import pallas as pl
from jax.experimental.pallas import tpu as pltpu
from jax.sharding import PartitionSpec as P

FEEDBACK_CUT = 0.25
STEP_SIZE = 0.1
EPSILON_SQ = 1e-06
PANEL = 32
PIECES = 2
LANES = 128

f32 = jnp.float32
bf16 = jnp.bfloat16


def split3(value):
    one = value.astype(bf16)
    rest = value - one.astype(f32)
    two = rest.astype(bf16)
    three = (rest - two.astype(f32)).astype(bf16)
    return one, two, three


IN_VMEM = pl.BlockSpec(memory_space=pltpu.VMEM)
ANYWHERE = pl.BlockSpec(memory_space=pltpu.HBM)
UNREAD = pl.BlockSpec(memory_space=pl.ANY)
BIG = pltpu.CompilerParams(vmem_limit_bytes=48 << 20)
SHORT = pl.CostEstimate(flops=1, bytes_accessed=1, transcendentals=0)


def eliminate(work, first):
    count, size = work.shape
    tiles = size // LANES

    @pl.loop(0, count // PANEL)
    def _(panel):
        top = pl.multiple_of(panel * PANEL, PANEL)
        left = pl.multiple_of(first + panel * PANEL, PANEL)
        tile = pl.multiple_of((left // LANES) * LANES, LANES)
        rows = work[pl.ds(top, PANEL), :]
        diag = pltpu.roll(
            work[pl.ds(top, PANEL), pl.ds(tile, LANES)], lax.rem(LANES - (left - tile), LANES), 1
        )
        lane = lax.broadcasted_iota(jnp.int32, (PANEL, size), 1)
        row = lax.broadcasted_iota(jnp.int32, (PANEL, size), 0)
        inside = (lane >= left) & (lane < left + PANEL)
        rows = jnp.where(inside, jnp.where(lane - left == row, 1.0, 0.0).astype(f32), rows)
        sub = lax.broadcasted_iota(jnp.int32, (PANEL, LANES), 0)
        cols = [
            jnp.broadcast_to(diag[k // 8 * 8 :, k : k + 1], (PANEL - k // 8 * 8, LANES))
            for k in range(PANEL)
        ]
        pivots = jnp.zeros((PANEL, LANES), f32)
        for j in range(PANEL):
            low = j // 8 * 8
            col = cols[j]
            pivot = col[j - low : j - low + 1, :]
            pivots = jnp.where(sub == j, pivot, pivots)
            if j == PANEL - 1:
                break
            factor = jnp.where(sub[low:] > j, col * (1.0 / pivot), 0.0)
            for k in range(j + 1, PANEL):
                cols[k] = cols[k] - col[k // 8 * 8 - low :, :] * factor[k - low : k - low + 1, :]
            step = jnp.concatenate([factor] * tiles, axis=1) * rows[j : j + 1, :]
            rows = jnp.concatenate([rows[:low], rows[low:] - step], axis=0) if low else rows - step
        scale = lax.rsqrt(pivots)
        scale = scale * (1.5 - 0.5 * pivots * scale * scale)
        rows = rows * jnp.concatenate([scale] * tiles, axis=1)
        work[pl.ds(top, PANEL), :] = rows
        lhs = stack_left(jnp.where(lane >= left + PANEL, rows, 0.0)[:, first:], 0)
        rhs = stack_right(rows, 0)
        for c in range(count // LANES):
            at = slice(c * LANES, (c + 1) * LANES)

            @pl.when((c + 1) * LANES > top + PANEL)
            def _():
                change = lax.dot_general(
                    lhs[:, at], rhs, (((0,), (0,)), ((), ())), preferred_element_type=f32
                )
                across = lax.broadcasted_iota(jnp.int32, (LANES, size), 1)
                down = lax.broadcasted_iota(jnp.int32, (LANES, size), 0) + c * LANES
                gone = (across >= left) & (across < left + PANEL) & (down >= top + PANEL)
                work[at, :] = jnp.where(gone, 0.0, work[at, :]) - change


def stack_left(value, axis):
    one, two, three = split3(value)
    return jnp.concatenate([one, one, two, one, two, three], axis=axis)


def stack_right(value, axis):
    one, two, three = split3(value)
    return jnp.concatenate([one, two, one, three, two, one], axis=axis)


def store_inverse(work, first, out_ref, one_ref, two_ref):
    across = lax.broadcasted_iota(jnp.int32, work.shape, 1)
    down = lax.broadcasted_iota(jnp.int32, work.shape, 0) + first
    inverse = jnp.where(across <= down, work[...], 0.0)
    one = inverse.astype(bf16)
    one_ref[...] = one
    two_ref[...] = (inverse - one.astype(f32)).astype(bf16)
    if out_ref is not None:
        out_ref[...] = inverse


def first_inverse_kernel(gram_ref, out_ref, one_ref, two_ref, work):
    work[...] = gram_ref[...]
    eliminate(work, 0)
    store_inverse(work, 0, out_ref, one_ref, two_ref)


def second_inverse_kernel(gram_ref, inverse_ref, _, one_ref, two_ref, work):
    first = inverse_ref.shape[0]
    inverse = inverse_ref[...]
    across = (((1,), (1,)), ((), ()))
    plain = (((1,), (0,)), ((), ()))
    low = lax.dot_general(
        stack_left(gram_ref[:, :first], 1), stack_right(inverse, 1), across, preferred_element_type=f32
    )
    low_left = stack_left(low, 1)
    work[:, :first] = -lax.dot_general(
        low_left, stack_right(inverse, 0), plain, preferred_element_type=f32
    )
    work[:, first:] = gram_ref[:, first:] - lax.dot_general(
        low_left, stack_right(low, 1), across, preferred_element_type=f32
    )
    eliminate(work, first)
    store_inverse(work, first, None, one_ref, two_ref)


def first_inverse(gram_mat):
    size = gram_mat.shape[0]
    return pl.pallas_call(
        first_inverse_kernel,
        out_shape=[
            jax.ShapeDtypeStruct((size, size), f32),
            jax.ShapeDtypeStruct((size, size), bf16),
            jax.ShapeDtypeStruct((size, size), bf16),
        ],
        in_specs=[pl.BlockSpec(memory_space=pltpu.VMEM)],
        out_specs=[pl.BlockSpec(memory_space=pltpu.VMEM)] * 3,
        scratch_shapes=[pltpu.VMEM((size, size), f32)],
        compiler_params=pltpu.CompilerParams(vmem_limit_bytes=24 << 20),
        cost_estimate=SHORT,
        name="first_inverse",
    )(gram_mat)


def second_inverse(gram_rows, inverse, earlier):
    shape = gram_rows.shape
    return pl.pallas_call(
        second_inverse_kernel,
        out_shape=[jax.ShapeDtypeStruct(shape, bf16)] * 2,
        in_specs=[IN_VMEM, IN_VMEM, UNREAD],
        out_specs=[pl.BlockSpec(memory_space=pltpu.VMEM)] * 2,
        scratch_shapes=[pltpu.VMEM(shape, f32)],
        compiler_params=pltpu.CompilerParams(vmem_limit_bytes=24 << 20),
        cost_estimate=SHORT,
        name="second_inverse",
    )(gram_rows, inverse, earlier)


def chunks_of(columns):
    wide = 512 if columns % LANES == 0 else columns
    return [(at, min(wide, columns - at)) for at in range(0, columns, wide)]


def copies(source, target, semaphores):
    return [
        pltpu.make_async_copy(source.at[:, pl.ds(at, wide)], target.at[:, pl.ds(at, wide)], semaphores.at[i])
        for i, (at, wide) in enumerate(chunks_of(source.shape[1]))
    ]


def back_kernel(count, has_ortho, _, *refs):
    left_refs, refs = refs[:count], refs[count:]
    one_ref, two_ref, refs = refs[0], refs[1], refs[2:]
    if has_ortho:
        earlier_ref, refs = refs[0], refs[1:]
    buffer_ref, ortho_ref, back_ref, held, arrived = refs
    coming = copies(buffer_ref, held, arrived)
    for copy in coming:
        copy.start()
    total = None
    at = 0
    for left_ref in left_refs:
        wide = left_ref.shape[1]
        for part in (one_ref, two_ref):
            term = lax.dot_general(
                left_ref[...], part[:, at : at + wide], (((1,), (1,)), ((), ())), preferred_element_type=f32
            )
            total = term if total is None else total + term
        at += wide
    if has_ortho:
        ortho_ref[:, : earlier_ref.shape[1]] = earlier_ref[...]
        ortho_ref[:, earlier_ref.shape[1] :] = total.astype(bf16)
    else:
        ortho_ref[...] = total.astype(bf16)
    turned = total.T.astype(bf16)
    for copy, (at, wide) in zip(coming, chunks_of(held.shape[1])):
        copy.wait()
        back_ref[:, at : at + wide] = jnp.dot(
            turned, held[:, at : at + wide], preferred_element_type=f32
        ).astype(bf16)


def back_product(before, lefts, one, two, earlier, buffer):
    rows, columns = buffer.shape
    rank = one.shape[0]
    extra = [] if earlier is None else [earlier]
    all_rank = rank + sum(v.shape[1] for v in extra)
    return pl.pallas_call(
        functools.partial(back_kernel, len(lefts), bool(extra)),
        out_shape=[
            jax.ShapeDtypeStruct((rows, all_rank), bf16),
            jax.ShapeDtypeStruct((rank, columns), bf16),
        ],
        in_specs=[UNREAD] + [IN_VMEM] * (len(lefts) + 2 + len(extra)) + [ANYWHERE],
        out_specs=[IN_VMEM, IN_VMEM],
        scratch_shapes=[
            pltpu.VMEM((rows, columns), bf16),
            pltpu.SemaphoreType.DMA((len(chunks_of(columns)),)),
        ],
        compiler_params=BIG,
        cost_estimate=SHORT,
        name="back_product",
    )(before, *lefts, one, two, *extra, buffer)


def pick_kernel(which_ref, part_ref, _, out_ref):
    rows = out_ref.shape[0]
    out_ref[...] = part_ref[pl.ds(pl.multiple_of(which_ref[0] * rows, rows), rows), :]


def pick(part, which, earlier):
    return pl.pallas_call(
        pick_kernel,
        out_shape=jax.ShapeDtypeStruct((part.shape[0] // 2, part.shape[1]), part.dtype),
        in_specs=[pl.BlockSpec(memory_space=pltpu.SMEM), IN_VMEM, UNREAD],
        out_specs=IN_VMEM,
        compiler_params=pltpu.CompilerParams(vmem_limit_bytes=16 << 20),
        cost_estimate=SHORT,
        name="pick",
    )(which.reshape(1).astype(jnp.int32), part, earlier)


def join_kernel(first_ref, own_ref, other_ref, _, out_ref):
    rows = own_ref.shape[0]
    at = first_ref[0]
    out_ref[pl.ds(pl.multiple_of(at * rows, rows), rows), :] = own_ref[...]
    out_ref[pl.ds(pl.multiple_of((1 - at) * rows, rows), rows), :] = other_ref[...]


def join(own, other, at, earlier):
    return pl.pallas_call(
        join_kernel,
        out_shape=jax.ShapeDtypeStruct((2 * own.shape[0], own.shape[1]), own.dtype),
        in_specs=[pl.BlockSpec(memory_space=pltpu.SMEM), IN_VMEM, IN_VMEM, UNREAD],
        out_specs=IN_VMEM,
        compiler_params=pltpu.CompilerParams(vmem_limit_bytes=16 << 20),
        cost_estimate=SHORT,
        name="join",
    )(at.reshape(1).astype(jnp.int32), own, other, earlier)


def total_kernel(*refs):
    *part_refs, _, out_ref = refs
    total = part_refs[0][...]
    for ref in part_refs[1:]:
        total = total + ref[...]
    out_ref[...] = total.astype(out_ref.dtype)


def total_of(parts, dtype, earlier):
    return pl.pallas_call(
        total_kernel,
        out_shape=jax.ShapeDtypeStruct(parts[0].shape, dtype),
        in_specs=[IN_VMEM] * len(parts) + [ANYWHERE],
        out_specs=IN_VMEM,
        compiler_params=pltpu.CompilerParams(vmem_limit_bytes=8 << 20),
        cost_estimate=SHORT,
        name="total",
    )(*parts, earlier)


def finish_kernel(own_ref, other_ref, _, out_ref, square_ref):
    total = own_ref[...].astype(f32) + other_ref[...].astype(f32)
    out_ref[...] = total.astype(bf16)
    square_ref[...] = jnp.broadcast_to(jnp.sum(total * total, axis=1, keepdims=True), square_ref.shape)


def finish(own, other, earlier):
    rows = own.shape[0]
    return pl.pallas_call(
        finish_kernel,
        out_shape=[jax.ShapeDtypeStruct(own.shape, bf16), jax.ShapeDtypeStruct((rows, LANES), f32)],
        in_specs=[IN_VMEM, IN_VMEM, UNREAD],
        out_specs=[IN_VMEM, IN_VMEM],
        compiler_params=pltpu.CompilerParams(vmem_limit_bytes=16 << 20),
        cost_estimate=SHORT,
        name="finish",
    )(own, other, earlier)


def update_kernel(cut, scaled, ortho_ref, *refs):
    back_refs, refs = refs[:PIECES], refs[PIECES:]
    if scaled:
        scale_refs, refs = refs[:PIECES], refs[PIECES:]
        value_ref, out_ref, right_ref, held, arrived, left, turned, turned_left = refs
    else:
        value_ref, out_ref, token_ref, held, arrived, left = refs
        token_ref[...] = jnp.zeros_like(token_ref)
    coming = copies(value_ref, held, arrived)
    going = copies(held, out_ref, left)
    for copy in coming:
        copy.start()
    rows, columns = held.shape
    tall = min(512, rows)
    leaving = []
    for i, (at, wide) in enumerate(chunks_of(columns)):
        backs = [ref[:, at : at + wide] for ref in back_refs]
        if scaled:
            rights = [v.astype(f32) * ref[...] for v, ref in zip(backs, scale_refs)]
            column = 0
            for v in rights:
                turned[at : at + wide, column : column + v.shape[0]] = v.T
                column += v.shape[0]
            copy = pltpu.make_async_copy(
                turned.at[pl.ds(at, wide), :], right_ref.at[pl.ds(at, wide), :], turned_left.at[i]
            )
            copy.start()
            leaving.append(copy)
            backs = [v.astype(bf16) for v in rights]
        back = jnp.concatenate(backs, axis=0)
        coming[i].wait()
        for top in range(0, rows, tall):
            here = (slice(top, top + tall), slice(at, at + wide))
            change = jnp.dot(ortho_ref[top : top + tall, :], back, preferred_element_type=f32)
            held[here] = (held[here].astype(f32) - cut * change).astype(bf16)
        going[i].start()
    for copy in going + leaving:
        copy.wait()


def update(cut, ortho, backs, scales, value, name):
    rows, columns = value.shape
    scaled = bool(scales)
    rank = sum(v.shape[0] for v in backs)
    count = len(chunks_of(columns))
    out_shape = [jax.ShapeDtypeStruct(value.shape, value.dtype)]
    scratch = [
        pltpu.VMEM((rows, columns), bf16),
        pltpu.SemaphoreType.DMA((count,)),
        pltpu.SemaphoreType.DMA((count,)),
    ]
    if scaled:
        out_shape.append(jax.ShapeDtypeStruct((columns, rank), f32))
        out_specs = [ANYWHERE] * 2
        scratch += [pltpu.VMEM((columns, rank), f32), pltpu.SemaphoreType.DMA((count,))]
    else:
        out_shape.append(jax.ShapeDtypeStruct((8, LANES), f32))
        out_specs = [ANYWHERE, IN_VMEM]
    return pl.pallas_call(
        functools.partial(update_kernel, cut, scaled),
        out_shape=out_shape,
        in_specs=[IN_VMEM] * (1 + len(backs) + len(scales)) + [ANYWHERE],
        out_specs=out_specs,
        scratch_shapes=scratch,
        compiler_params=BIG,
        cost_estimate=SHORT,
        name=name,
    )(ortho, *backs, *scales, value)


def swap(value, axis, count, bit):
    return lax.ppermute(value, axis, [(i, i ^ bit) for i in range(count)])


def take(value, part, parts):
    share = value.shape[0] // parts
    return lax.dynamic_slice_in_dim(value, part * share, share, 0)


def in_order(first, own, other):
    return jnp.concatenate([jnp.where(first, own, other), jnp.where(first, other, own)], axis=0)


def make_on_device(n_row, n_col):
    n_line = n_col // 2

    def along(value, steps):
        return lax.ppermute(
            value, "col", [(i, (i // 2 + steps) % n_line * 2 + i % 2) for i in range(n_col)]
        )

    def on_device(weight, momentum, grad, right_factor):
        full = right_factor.shape[0] * n_col
        core = lax.axis_index("row") % 2
        side = lax.axis_index("col") % 2
        place = lax.axis_index("col") // 2

        def reduce_pair(part):
            sent = take(part, 1 - side, 2).astype(bf16)
            return take(part, side, 2) + swap(sent, "col", n_col, 1).astype(f32)

        def reduce_line(part):
            total = take(part, place, n_line)
            for d in range(1, n_line):
                total = total + along(
                    take(part, (place + d) % n_line, n_line).astype(bf16), d
                ).astype(f32)
            return total.astype(bf16)

        def gather_line(share):
            rows = share.shape[0]
            joined = jnp.zeros((n_line * rows, share.shape[1]), bf16)
            joined = lax.dynamic_update_slice_in_dim(joined, share, place * rows, 0)
            for d in range(1, n_line):
                at = (place + n_line - d) % n_line * rows
                joined = lax.dynamic_update_slice_in_dim(joined, along(share, d), at, 0)
            return joined

        def gather_pair(half):
            return in_order(side == 0, half, swap(half, "col", n_col, 1))

        def sum_cores(part):
            return take(part, core, 2) + swap(take(part, 1 - core, 2), "row", n_row, 1)

        def sum_others(half):
            bit = 2
            while bit < n_row:
                half = half + swap(half, "row", n_row, bit)
                bit *= 2
            return half

        def join_cores(half):
            return in_order(core == 0, half, swap(half, "row", n_row, 1))

        def sum_core(part, sent):
            own = take(part, core, 2).astype(f32) + swap(sent, "row", n_row, 1).astype(f32)
            return own.astype(bf16)

        def sum_chips(own, earlier):
            bit = 2
            while 2 * bit < n_row:
                own = (own.astype(f32) + swap(own, "row", n_row, bit).astype(f32)).astype(bf16)
                bit *= 2
            total, squares = finish(own, swap(own, "row", n_row, bit), earlier)
            return total, squares[:, :1].reshape(1, -1)

        def sum_squares(squares, meanwhile):
            squares = squares + swap(squares, "col", n_col, 1)
            others = [along(squares, d) for d in range(1, n_line)]
            squares = total_of([squares, *others], f32, meanwhile)
            return in_order(core == 0, squares, swap(squares, "row", n_row, 1))

        buffer = (momentum.astype(f32) + grad.astype(f32)).astype(bf16)
        right_in = right_factor.astype(bf16)
        piece = right_in.shape[1] // 2
        part_1 = jnp.dot(buffer, right_in[:, :piece], preferred_element_type=f32)
        part_2 = jnp.dot(buffer, right_in[:, piece:], preferred_element_type=f32)
        over_rows = (((0,), (0,)), ((), ()))

        pair_1 = reduce_pair(part_1)
        share_1 = reduce_line(pair_1)
        pair_2 = reduce_pair(part_2)
        line_1 = gather_line(share_1)
        share_2 = reduce_line(pair_2)
        left_1 = gather_pair(line_1)
        line_2 = gather_line(share_2)
        gram_1 = join_cores(
            sum_others(
                sum_cores(lax.dot_general(left_1, left_1, over_rows, preferred_element_type=f32))
            )
        )
        inverse_1, one_1, two_1 = first_inverse(gram_1)
        left_2 = join(line_2, swap(line_2, "col", n_col, 1), side, inverse_1)
        gram_2 = sum_cores(
            jnp.concatenate(
                [
                    lax.dot_general(left_2, left_1, over_rows, preferred_element_type=f32),
                    lax.dot_general(left_2, left_2, over_rows, preferred_element_type=f32),
                ],
                axis=1,
            )
        )
        ortho_1, back_part_1 = back_product(gram_2, [left_1], one_1, two_1, None, buffer)
        gram_2 = sum_others(gram_2)
        core_1 = sum_core(back_part_1, pick(back_part_1, 1 - core, gram_2))
        chips_1, squares_1 = sum_chips(core_1, core_1)
        one_2, two_2 = second_inverse(join_cores(gram_2), inverse_1, core_1)
        ortho, back_part_2 = back_product(core_1, [left_1, left_2], one_2, two_2, ortho_1, buffer)
        core_2 = sum_core(back_part_2, pick(back_part_2, 1 - core, chips_1))
        chips_2, squares_2 = sum_chips(core_2, core_2)
        back_1 = join_cores(chips_1)
        back_2 = join_cores(chips_2)
        momentum_next, token = update(FEEDBACK_CUT, ortho, [back_1, back_2], [], buffer, "momentum_update")
        squares = jnp.concatenate([squares_1, squares_2], axis=1).reshape(2, -1)
        squares = sum_squares(squares, token)
        squares = jnp.concatenate([squares[0:1], squares[2:3], squares[1:2], squares[3:4]], axis=0).reshape(2, piece, 1)
        scale = jnp.sqrt(f32(full)) / jnp.sqrt(squares + EPSILON_SQ)

        weight_next, right_next = update(
            STEP_SIZE, ortho, [back_1, back_2], [scale[0], scale[1]], weight, "weight_update"
        )
        return (weight_next, momentum_next, right_next)

    return on_device


def solution(mesh):
    in_specs = (P("row", "col"), P("row", "col"), P("row", "col"), P("col", None))
    out_specs = (P("row", "col"), P("row", "col"), P("col", None))
    return jax.shard_map(
        make_on_device(mesh.shape["row"], mesh.shape["col"]),
        mesh=mesh,
        in_specs=in_specs,
        out_specs=out_specs,
        check_vma=False,
    )
```

```python
import functools

import jax
import jax.numpy as jnp
from jax import lax
from jax.experimental import pallas as pl
from jax.experimental.pallas import tpu as pltpu
from jax.sharding import PartitionSpec as P

FEEDBACK_CUT = 0.25
STEP_SIZE = 0.1
EPSILON_SQ = 1e-06
PANEL = 32
PIECES = 2
LANES = 128

f32 = jnp.float32
bf16 = jnp.bfloat16


def split3(value):
    one = value.astype(bf16)
    rest = value - one.astype(f32)
    two = rest.astype(bf16)
    three = (rest - two.astype(f32)).astype(bf16)
    return one, two, three


IN_VMEM = pl.BlockSpec(memory_space=pltpu.VMEM)
ANYWHERE = pl.BlockSpec(memory_space=pltpu.HBM)
UNREAD = pl.BlockSpec(memory_space=pl.ANY)
BIG = pltpu.CompilerParams(vmem_limit_bytes=48 << 20)
SHORT = pl.CostEstimate(flops=1, bytes_accessed=1, transcendentals=0)


def eliminate(work, first):
    count, size = work.shape
    tiles = size // LANES

    @pl.loop(0, count // PANEL)
    def _(panel):
        top = pl.multiple_of(panel * PANEL, PANEL)
        left = pl.multiple_of(first + panel * PANEL, PANEL)
        tile = pl.multiple_of((left // LANES) * LANES, LANES)
        rows = work[pl.ds(top, PANEL), :]
        diag = pltpu.roll(
            work[pl.ds(top, PANEL), pl.ds(tile, LANES)], lax.rem(LANES - (left - tile), LANES), 1
        )
        lane = lax.broadcasted_iota(jnp.int32, (PANEL, size), 1)
        row = lax.broadcasted_iota(jnp.int32, (PANEL, size), 0)
        inside = (lane >= left) & (lane < left + PANEL)
        rows = jnp.where(inside, jnp.where(lane - left == row, 1.0, 0.0).astype(f32), rows)
        sub = lax.broadcasted_iota(jnp.int32, (PANEL, LANES), 0)
        cols = [
            jnp.broadcast_to(diag[k // 8 * 8 :, k : k + 1], (PANEL - k // 8 * 8, LANES))
            for k in range(PANEL)
        ]
        pivots = jnp.zeros((PANEL, LANES), f32)
        for j in range(PANEL):
            low = j // 8 * 8
            col = cols[j]
            pivot = col[j - low : j - low + 1, :]
            pivots = jnp.where(sub == j, pivot, pivots)
            if j == PANEL - 1:
                break
            factor = jnp.where(sub[low:] > j, col * (1.0 / pivot), 0.0)
            for k in range(j + 1, PANEL):
                cols[k] = cols[k] - col[k // 8 * 8 - low :, :] * factor[k - low : k - low + 1, :]
            step = jnp.concatenate([factor] * tiles, axis=1) * rows[j : j + 1, :]
            rows = jnp.concatenate([rows[:low], rows[low:] - step], axis=0) if low else rows - step
        scale = lax.rsqrt(pivots)
        scale = scale * (1.5 - 0.5 * pivots * scale * scale)
        rows = rows * jnp.concatenate([scale] * tiles, axis=1)
        work[pl.ds(top, PANEL), :] = rows
        lhs = stack_left(jnp.where(lane >= left + PANEL, rows, 0.0)[:, first:], 0)
        rhs = stack_right(rows, 0)
        for c in range(count // LANES):
            at = slice(c * LANES, (c + 1) * LANES)

            @pl.when((c + 1) * LANES > top + PANEL)
            def _():
                change = lax.dot_general(
                    lhs[:, at], rhs, (((0,), (0,)), ((), ())), preferred_element_type=f32
                )
                across = lax.broadcasted_iota(jnp.int32, (LANES, size), 1)
                down = lax.broadcasted_iota(jnp.int32, (LANES, size), 0) + c * LANES
                gone = (across >= left) & (across < left + PANEL) & (down >= top + PANEL)
                work[at, :] = jnp.where(gone, 0.0, work[at, :]) - change


def stack_left(value, axis):
    one, two, three = split3(value)
    return jnp.concatenate([one, one, two, one, two, three], axis=axis)


def stack_right(value, axis):
    one, two, three = split3(value)
    return jnp.concatenate([one, two, one, three, two, one], axis=axis)


def store_inverse(work, first, out_ref, one_ref, two_ref):
    across = lax.broadcasted_iota(jnp.int32, work.shape, 1)
    down = lax.broadcasted_iota(jnp.int32, work.shape, 0) + first
    inverse = jnp.where(across <= down, work[...], 0.0)
    one = inverse.astype(bf16)
    one_ref[...] = one
    two_ref[...] = (inverse - one.astype(f32)).astype(bf16)
    if out_ref is not None:
        out_ref[...] = inverse


def first_inverse_kernel(gram_ref, out_ref, one_ref, two_ref, work):
    work[...] = gram_ref[...]
    eliminate(work, 0)
    store_inverse(work, 0, out_ref, one_ref, two_ref)


def second_inverse_kernel(gram_ref, inverse_ref, _, one_ref, two_ref, work):
    first = inverse_ref.shape[0]
    inverse = inverse_ref[...]
    across = (((1,), (1,)), ((), ()))
    plain = (((1,), (0,)), ((), ()))
    low = lax.dot_general(
        stack_left(gram_ref[:, :first], 1), stack_right(inverse, 1), across, preferred_element_type=f32
    )
    low_left = stack_left(low, 1)
    work[:, :first] = -lax.dot_general(
        low_left, stack_right(inverse, 0), plain, preferred_element_type=f32
    )
    work[:, first:] = gram_ref[:, first:] - lax.dot_general(
        low_left, stack_right(low, 1), across, preferred_element_type=f32
    )
    eliminate(work, first)
    store_inverse(work, first, None, one_ref, two_ref)


def first_inverse(gram_mat):
    size = gram_mat.shape[0]
    return pl.pallas_call(
        first_inverse_kernel,
        out_shape=[
            jax.ShapeDtypeStruct((size, size), f32),
            jax.ShapeDtypeStruct((size, size), bf16),
            jax.ShapeDtypeStruct((size, size), bf16),
        ],
        in_specs=[pl.BlockSpec(memory_space=pltpu.VMEM)],
        out_specs=[pl.BlockSpec(memory_space=pltpu.VMEM)] * 3,
        scratch_shapes=[pltpu.VMEM((size, size), f32)],
        compiler_params=pltpu.CompilerParams(vmem_limit_bytes=24 << 20),
        cost_estimate=SHORT,
        name="first_inverse",
    )(gram_mat)


def second_inverse(gram_rows, inverse, earlier):
    shape = gram_rows.shape
    return pl.pallas_call(
        second_inverse_kernel,
        out_shape=[jax.ShapeDtypeStruct(shape, bf16)] * 2,
        in_specs=[IN_VMEM, IN_VMEM, UNREAD],
        out_specs=[pl.BlockSpec(memory_space=pltpu.VMEM)] * 2,
        scratch_shapes=[pltpu.VMEM(shape, f32)],
        compiler_params=pltpu.CompilerParams(vmem_limit_bytes=24 << 20),
        cost_estimate=SHORT,
        name="second_inverse",
    )(gram_rows, inverse, earlier)


def chunks_of(columns):
    wide = 512 if columns % LANES == 0 else columns
    return [(at, min(wide, columns - at)) for at in range(0, columns, wide)]


def copies(source, target, semaphores):
    return [
        pltpu.make_async_copy(source.at[:, pl.ds(at, wide)], target.at[:, pl.ds(at, wide)], semaphores.at[i])
        for i, (at, wide) in enumerate(chunks_of(source.shape[1]))
    ]


def back_kernel(count, has_ortho, _, *refs):
    left_refs, refs = refs[:count], refs[count:]
    one_ref, two_ref, refs = refs[0], refs[1], refs[2:]
    if has_ortho:
        earlier_ref, refs = refs[0], refs[1:]
    buffer_ref, ortho_ref, back_ref, held, arrived = refs
    coming = copies(buffer_ref, held, arrived)
    for copy in coming:
        copy.start()
    left = [ref[...] for ref in left_refs]
    total = lax.dot_general(
        jnp.concatenate(left + left, axis=1),
        jnp.concatenate([one_ref[...], two_ref[...]], axis=1),
        (((1,), (1,)), ((), ())),
        preferred_element_type=f32,
    )
    if has_ortho:
        ortho_ref[:, : earlier_ref.shape[1]] = earlier_ref[...]
        ortho_ref[:, earlier_ref.shape[1] :] = total.astype(bf16)
    else:
        ortho_ref[...] = total.astype(bf16)
    turned = total.T.astype(bf16)
    for copy, (at, wide) in zip(coming, chunks_of(held.shape[1])):
        copy.wait()
        back_ref[:, at : at + wide] = jnp.dot(
            turned, held[:, at : at + wide], preferred_element_type=f32
        ).astype(bf16)


def back_product(before, lefts, one, two, earlier, buffer):
    rows, columns = buffer.shape
    rank = one.shape[0]
    extra = [] if earlier is None else [earlier]
    all_rank = rank + sum(v.shape[1] for v in extra)
    return pl.pallas_call(
        functools.partial(back_kernel, len(lefts), bool(extra)),
        out_shape=[
            jax.ShapeDtypeStruct((rows, all_rank), bf16),
            jax.ShapeDtypeStruct((rank, columns), bf16),
        ],
        in_specs=[UNREAD] + [IN_VMEM] * (len(lefts) + 2 + len(extra)) + [ANYWHERE],
        out_specs=[IN_VMEM, IN_VMEM],
        scratch_shapes=[
            pltpu.VMEM((rows, columns), bf16),
            pltpu.SemaphoreType.DMA((len(chunks_of(columns)),)),
        ],
        compiler_params=BIG,
        cost_estimate=SHORT,
        name="back_product",
    )(before, *lefts, one, two, *extra, buffer)


def pick_kernel(which_ref, part_ref, _, out_ref):
    rows = out_ref.shape[0]
    out_ref[...] = part_ref[pl.ds(pl.multiple_of(which_ref[0] * rows, rows), rows), :]


def pick(part, which, earlier):
    return pl.pallas_call(
        pick_kernel,
        out_shape=jax.ShapeDtypeStruct((part.shape[0] // 2, part.shape[1]), part.dtype),
        in_specs=[pl.BlockSpec(memory_space=pltpu.SMEM), IN_VMEM, UNREAD],
        out_specs=IN_VMEM,
        compiler_params=pltpu.CompilerParams(vmem_limit_bytes=16 << 20),
        cost_estimate=SHORT,
        name="pick",
    )(which.reshape(1).astype(jnp.int32), part, earlier)


def join_kernel(first_ref, own_ref, other_ref, _, out_ref):
    rows = own_ref.shape[0]
    at = first_ref[0]
    out_ref[pl.ds(pl.multiple_of(at * rows, rows), rows), :] = own_ref[...]
    out_ref[pl.ds(pl.multiple_of((1 - at) * rows, rows), rows), :] = other_ref[...]


def join(own, other, at, earlier):
    return pl.pallas_call(
        join_kernel,
        out_shape=jax.ShapeDtypeStruct((2 * own.shape[0], own.shape[1]), own.dtype),
        in_specs=[pl.BlockSpec(memory_space=pltpu.SMEM), IN_VMEM, IN_VMEM, UNREAD],
        out_specs=IN_VMEM,
        compiler_params=pltpu.CompilerParams(vmem_limit_bytes=16 << 20),
        cost_estimate=SHORT,
        name="join",
    )(at.reshape(1).astype(jnp.int32), own, other, earlier)


def total_kernel(*refs):
    *part_refs, _, out_ref = refs
    total = part_refs[0][...]
    for ref in part_refs[1:]:
        total = total + ref[...]
    out_ref[...] = total.astype(out_ref.dtype)


def total_of(parts, dtype, earlier):
    return pl.pallas_call(
        total_kernel,
        out_shape=jax.ShapeDtypeStruct(parts[0].shape, dtype),
        in_specs=[IN_VMEM] * len(parts) + [ANYWHERE],
        out_specs=IN_VMEM,
        compiler_params=pltpu.CompilerParams(vmem_limit_bytes=8 << 20),
        cost_estimate=SHORT,
        name="total",
    )(*parts, earlier)


def finish_kernel(own_ref, other_ref, _, out_ref, square_ref):
    total = own_ref[...].astype(f32) + other_ref[...].astype(f32)
    out_ref[...] = total.astype(bf16)
    square_ref[...] = jnp.broadcast_to(jnp.sum(total * total, axis=1, keepdims=True), square_ref.shape)


def finish(own, other, earlier):
    rows = own.shape[0]
    return pl.pallas_call(
        finish_kernel,
        out_shape=[jax.ShapeDtypeStruct(own.shape, bf16), jax.ShapeDtypeStruct((rows, LANES), f32)],
        in_specs=[IN_VMEM, IN_VMEM, UNREAD],
        out_specs=[IN_VMEM, IN_VMEM],
        compiler_params=pltpu.CompilerParams(vmem_limit_bytes=16 << 20),
        cost_estimate=SHORT,
        name="finish",
    )(own, other, earlier)


def update_kernel(cut, scaled, ortho_ref, *refs):
    back_refs, refs = refs[:PIECES], refs[PIECES:]
    if scaled:
        scale_ref, refs = refs[0], refs[1:]
        upright = scale_ref[...].T
        scales = [
            jnp.concatenate([upright[:, p : p + 1], upright[:, PIECES + p : PIECES + p + 1]], axis=0)
            for p in range(PIECES)
        ]
        value_ref, out_ref, right_ref, held, arrived, left, turned, turned_left = refs
    else:
        value_ref, out_ref, token_ref, held, arrived, left = refs
        token_ref[...] = jnp.zeros_like(token_ref)
    coming = copies(value_ref, held, arrived)
    going = copies(held, out_ref, left)
    for copy in coming:
        copy.start()
    rows, columns = held.shape
    tall = min(512, rows)
    leaving = []
    for i, (at, wide) in enumerate(chunks_of(columns)):
        backs = [ref[:, at : at + wide] for ref in back_refs]
        if scaled:
            rights = [v.astype(f32) * by for v, by in zip(backs, scales)]
            column = 0
            for v in rights:
                turned[at : at + wide, column : column + v.shape[0]] = v.T
                column += v.shape[0]
            copy = pltpu.make_async_copy(
                turned.at[pl.ds(at, wide), :], right_ref.at[pl.ds(at, wide), :], turned_left.at[i]
            )
            copy.start()
            leaving.append(copy)
            backs = [v.astype(bf16) for v in rights]
        back = jnp.concatenate(backs, axis=0)
        coming[i].wait()
        for top in range(0, rows, tall):
            here = (slice(top, top + tall), slice(at, at + wide))
            change = jnp.dot(ortho_ref[top : top + tall, :], back, preferred_element_type=f32)
            held[here] = (held[here].astype(f32) - cut * change).astype(bf16)
        going[i].start()
    for copy in going + leaving:
        copy.wait()


def update(cut, ortho, backs, scales, value, name):
    rows, columns = value.shape
    scaled = bool(scales)
    rank = sum(v.shape[0] for v in backs)
    count = len(chunks_of(columns))
    out_shape = [jax.ShapeDtypeStruct(value.shape, value.dtype)]
    scratch = [
        pltpu.VMEM((rows, columns), bf16),
        pltpu.SemaphoreType.DMA((count,)),
        pltpu.SemaphoreType.DMA((count,)),
    ]
    if scaled:
        out_shape.append(jax.ShapeDtypeStruct((columns, rank), f32))
        out_specs = [ANYWHERE] * 2
        scratch += [pltpu.VMEM((columns, rank), f32), pltpu.SemaphoreType.DMA((count,))]
    else:
        out_shape.append(jax.ShapeDtypeStruct((8, LANES), f32))
        out_specs = [ANYWHERE, IN_VMEM]
    return pl.pallas_call(
        functools.partial(update_kernel, cut, scaled),
        out_shape=out_shape,
        in_specs=[IN_VMEM] * (1 + len(backs) + len(scales)) + [ANYWHERE],
        out_specs=out_specs,
        scratch_shapes=scratch,
        compiler_params=pltpu.CompilerParams(vmem_limit_bytes=36 << 20),
        cost_estimate=SHORT,
        name=name,
    )(ortho, *backs, *scales, value)


def swap(value, axis, count, bit):
    return lax.ppermute(value, axis, [(i, i ^ bit) for i in range(count)])


def take(value, part, parts):
    share = value.shape[0] // parts
    return lax.dynamic_slice_in_dim(value, part * share, share, 0)


def in_order(first, own, other):
    return jnp.concatenate([jnp.where(first, own, other), jnp.where(first, other, own)], axis=0)


def make_on_device(n_row, n_col):
    n_line = n_col // 2

    def along(value, steps):
        return lax.ppermute(
            value, "col", [(i, (i // 2 + steps) % n_line * 2 + i % 2) for i in range(n_col)]
        )

    def on_device(weight, momentum, grad, right_factor):
        full = right_factor.shape[0] * n_col
        core = lax.axis_index("row") % 2
        side = lax.axis_index("col") % 2
        place = lax.axis_index("col") // 2

        def reduce_pair(part):
            sent = take(part, 1 - side, 2).astype(bf16)
            return take(part, side, 2) + swap(sent, "col", n_col, 1).astype(f32)

        def reduce_line(part):
            total = take(part, place, n_line)
            for d in range(1, n_line):
                total = total + along(
                    take(part, (place + d) % n_line, n_line).astype(bf16), d
                ).astype(f32)
            return total.astype(bf16)

        def gather_line(share):
            rows = share.shape[0]
            joined = jnp.zeros((n_line * rows, share.shape[1]), bf16)
            joined = lax.dynamic_update_slice_in_dim(joined, share, place * rows, 0)
            for d in range(1, n_line):
                at = (place + n_line - d) % n_line * rows
                joined = lax.dynamic_update_slice_in_dim(joined, along(share, d), at, 0)
            return joined

        def gather_pair(half):
            return in_order(side == 0, half, swap(half, "col", n_col, 1))

        def sum_cores(part):
            return take(part, core, 2) + swap(take(part, 1 - core, 2), "row", n_row, 1)

        def sum_others(half):
            bit = 2
            while bit < n_row:
                half = half + swap(half, "row", n_row, bit)
                bit *= 2
            return half

        def join_cores(half):
            return in_order(core == 0, half, swap(half, "row", n_row, 1))

        def sum_core(part, sent):
            own = take(part, core, 2).astype(f32) + swap(sent, "row", n_row, 1).astype(f32)
            return own.astype(bf16)

        def sum_chips(own, earlier):
            bit = 2
            while 2 * bit < n_row:
                own = (own.astype(f32) + swap(own, "row", n_row, bit).astype(f32)).astype(bf16)
                bit *= 2
            total, squares = finish(own, swap(own, "row", n_row, bit), earlier)
            return total, squares[:, :1].reshape(1, -1)

        def sum_squares(squares, meanwhile):
            squares = squares + swap(squares, "col", n_col, 1)
            others = [along(squares, d) for d in range(1, n_line)]
            squares = total_of([squares, *others], f32, meanwhile)
            return in_order(core == 0, squares, swap(squares, "row", n_row, 1))

        buffer = (momentum.astype(f32) + grad.astype(f32)).astype(bf16)
        right_in = right_factor.astype(bf16)
        piece = right_in.shape[1] // 2
        part_1 = jnp.dot(buffer, right_in[:, :piece], preferred_element_type=f32)
        part_2 = jnp.dot(buffer, right_in[:, piece:], preferred_element_type=f32)
        over_rows = (((0,), (0,)), ((), ()))

        pair_1 = reduce_pair(part_1)
        share_1 = reduce_line(pair_1)
        pair_2 = reduce_pair(part_2)
        line_1 = gather_line(share_1)
        share_2 = reduce_line(pair_2)
        left_1 = gather_pair(line_1)
        line_2 = gather_line(share_2)
        gram_1 = join_cores(
            sum_others(
                sum_cores(lax.dot_general(left_1, left_1, over_rows, preferred_element_type=f32))
            )
        )
        inverse_1, one_1, two_1 = first_inverse(gram_1)
        left_2 = join(line_2, swap(line_2, "col", n_col, 1), side, inverse_1)
        gram_2 = sum_cores(
            jnp.concatenate(
                [
                    lax.dot_general(left_2, left_1, over_rows, preferred_element_type=f32),
                    lax.dot_general(left_2, left_2, over_rows, preferred_element_type=f32),
                ],
                axis=1,
            )
        )
        ortho_1, back_part_1 = back_product(gram_2, [left_1], one_1, two_1, None, buffer)
        gram_2 = sum_others(gram_2)
        core_1 = sum_core(back_part_1, pick(back_part_1, 1 - core, gram_2))
        chips_1, squares_1 = sum_chips(core_1, core_1)
        one_2, two_2 = second_inverse(join_cores(gram_2), inverse_1, core_1)
        ortho, back_part_2 = back_product(core_1, [left_1, left_2], one_2, two_2, ortho_1, buffer)
        core_2 = sum_core(back_part_2, pick(back_part_2, 1 - core, chips_1))
        chips_2, squares_2 = sum_chips(core_2, core_2)
        back_1 = join_cores(chips_1)
        back_2 = join_cores(chips_2)
        momentum_next, token = update(FEEDBACK_CUT, ortho, [back_1, back_2], [], buffer, "momentum_update")
        squares = jnp.concatenate([squares_1, squares_2], axis=1).reshape(2, -1)
        squares = sum_squares(squares, token)
        squares = jnp.concatenate([squares, squares], axis=0)
        scale = jnp.sqrt(f32(full)) / jnp.sqrt(squares + EPSILON_SQ)

        weight_next, right_next = update(
            STEP_SIZE, ortho, [back_1, back_2], [scale], weight, "weight_update"
        )
        return (weight_next, momentum_next, right_next)

    return on_device


def solution(mesh):
    in_specs = (P("row", "col"), P("row", "col"), P("row", "col"), P("col", None))
    out_specs = (P("row", "col"), P("row", "col"), P("col", None))
    return jax.shard_map(
        make_on_device(mesh.shape["row"], mesh.shape["col"]),
        mesh=mesh,
        in_specs=in_specs,
        out_specs=out_specs,
        check_vma=False,
    )
```

```python
import functools

import jax
import jax.numpy as jnp
from jax import lax
from jax.experimental import pallas as pl
from jax.experimental.pallas import tpu as pltpu
from jax.sharding import PartitionSpec as P

FEEDBACK_CUT = 0.25
STEP_SIZE = 0.1
EPSILON_SQ = 1e-06
PANEL = 32
PIECES = 2
LANES = 128

f32 = jnp.float32
bf16 = jnp.bfloat16


def split3(value):
    one = value.astype(bf16)
    rest = value - one.astype(f32)
    two = rest.astype(bf16)
    three = (rest - two.astype(f32)).astype(bf16)
    return one, two, three


IN_VMEM = pl.BlockSpec(memory_space=pltpu.VMEM)
ANYWHERE = pl.BlockSpec(memory_space=pltpu.HBM)
UNREAD = pl.BlockSpec(memory_space=pl.ANY)
BIG = pltpu.CompilerParams(vmem_limit_bytes=32 << 20)
SHORT = pl.CostEstimate(flops=1, bytes_accessed=1, transcendentals=0)


def eliminate(work, first):
    count, size = work.shape
    tiles = size // LANES

    @pl.loop(0, count // PANEL)
    def _(panel):
        top = pl.multiple_of(panel * PANEL, PANEL)
        left = pl.multiple_of(first + panel * PANEL, PANEL)
        tile = pl.multiple_of((left // LANES) * LANES, LANES)
        rows = work[pl.ds(top, PANEL), :]
        diag = pltpu.roll(
            work[pl.ds(top, PANEL), pl.ds(tile, LANES)], lax.rem(LANES - (left - tile), LANES), 1
        )
        lane = lax.broadcasted_iota(jnp.int32, (PANEL, size), 1)
        row = lax.broadcasted_iota(jnp.int32, (PANEL, size), 0)
        inside = (lane >= left) & (lane < left + PANEL)
        rows = jnp.where(inside, jnp.where(lane - left == row, 1.0, 0.0).astype(f32), rows)
        sub = lax.broadcasted_iota(jnp.int32, (PANEL, LANES), 0)
        cols = [
            jnp.broadcast_to(diag[k // 8 * 8 :, k : k + 1], (PANEL - k // 8 * 8, LANES))
            for k in range(PANEL)
        ]
        pivots = jnp.zeros((PANEL, LANES), f32)
        for j in range(PANEL):
            low = j // 8 * 8
            col = cols[j]
            pivot = col[j - low : j - low + 1, :]
            pivots = jnp.where(sub == j, pivot, pivots)
            if j == PANEL - 1:
                break
            factor = jnp.where(sub[low:] > j, col * (1.0 / pivot), 0.0)
            for k in range(j + 1, PANEL):
                cols[k] = cols[k] - col[k // 8 * 8 - low :, :] * factor[k - low : k - low + 1, :]
            step = jnp.concatenate([factor] * tiles, axis=1) * rows[j : j + 1, :]
            rows = jnp.concatenate([rows[:low], rows[low:] - step], axis=0) if low else rows - step
        scale = lax.rsqrt(pivots)
        scale = scale * (1.5 - 0.5 * pivots * scale * scale)
        rows = rows * jnp.concatenate([scale] * tiles, axis=1)
        work[pl.ds(top, PANEL), :] = rows
        lhs = stack_left(jnp.where(lane >= left + PANEL, rows, 0.0)[:, first:], 0)
        rhs = stack_right(rows, 0)
        for c in range(count // LANES):
            at = slice(c * LANES, (c + 1) * LANES)

            @pl.when((c + 1) * LANES > top + PANEL)
            def _():
                change = lax.dot_general(
                    lhs[:, at], rhs, (((0,), (0,)), ((), ())), preferred_element_type=f32
                )
                across = lax.broadcasted_iota(jnp.int32, (LANES, size), 1)
                down = lax.broadcasted_iota(jnp.int32, (LANES, size), 0) + c * LANES
                gone = (across >= left) & (across < left + PANEL) & (down >= top + PANEL)
                work[at, :] = jnp.where(gone, 0.0, work[at, :]) - change


def stack_left(value, axis):
    one, two, three = split3(value)
    return jnp.concatenate([one, one, two, one, two, three], axis=axis)


def stack_right(value, axis):
    one, two, three = split3(value)
    return jnp.concatenate([one, two, one, three, two, one], axis=axis)


def store_inverse(work, first, out_ref, one_ref, two_ref):
    across = lax.broadcasted_iota(jnp.int32, work.shape, 1)
    down = lax.broadcasted_iota(jnp.int32, work.shape, 0) + first
    inverse = jnp.where(across <= down, work[...], 0.0)
    one = inverse.astype(bf16)
    one_ref[...] = one
    two_ref[...] = (inverse - one.astype(f32)).astype(bf16)
    if out_ref is not None:
        out_ref[...] = inverse


def first_inverse_kernel(gram_ref, out_ref, one_ref, two_ref, work):
    work[...] = gram_ref[...]
    eliminate(work, 0)
    store_inverse(work, 0, out_ref, one_ref, two_ref)


def second_inverse_kernel(gram_ref, inverse_ref, _, one_ref, two_ref, work):
    first = inverse_ref.shape[0]
    inverse = inverse_ref[...]
    across = (((1,), (1,)), ((), ()))
    plain = (((1,), (0,)), ((), ()))
    low = lax.dot_general(
        stack_left(gram_ref[:, :first], 1), stack_right(inverse, 1), across, preferred_element_type=f32
    )
    low_left = stack_left(low, 1)
    work[:, :first] = -lax.dot_general(
        low_left, stack_right(inverse, 0), plain, preferred_element_type=f32
    )
    work[:, first:] = gram_ref[:, first:] - lax.dot_general(
        low_left, stack_right(low, 1), across, preferred_element_type=f32
    )
    eliminate(work, first)
    store_inverse(work, first, None, one_ref, two_ref)


def first_inverse(gram_mat):
    size = gram_mat.shape[0]
    return pl.pallas_call(
        first_inverse_kernel,
        out_shape=[
            jax.ShapeDtypeStruct((size, size), f32),
            jax.ShapeDtypeStruct((size, size), bf16),
            jax.ShapeDtypeStruct((size, size), bf16),
        ],
        in_specs=[pl.BlockSpec(memory_space=pltpu.VMEM)],
        out_specs=[pl.BlockSpec(memory_space=pltpu.VMEM)] * 3,
        scratch_shapes=[pltpu.VMEM((size, size), f32)],
        compiler_params=pltpu.CompilerParams(vmem_limit_bytes=24 << 20),
        cost_estimate=SHORT,
        name="first_inverse",
    )(gram_mat)


def second_inverse(gram_rows, inverse, earlier):
    shape = gram_rows.shape
    return pl.pallas_call(
        second_inverse_kernel,
        out_shape=[jax.ShapeDtypeStruct(shape, bf16)] * 2,
        in_specs=[IN_VMEM, IN_VMEM, UNREAD],
        out_specs=[pl.BlockSpec(memory_space=pltpu.VMEM)] * 2,
        scratch_shapes=[pltpu.VMEM(shape, f32)],
        compiler_params=pltpu.CompilerParams(vmem_limit_bytes=24 << 20),
        cost_estimate=SHORT,
        name="second_inverse",
    )(gram_rows, inverse, earlier)


def chunks_of(columns):
    wide = 512 if columns % LANES == 0 else columns
    return [(at, min(wide, columns - at)) for at in range(0, columns, wide)]


def copies(source, target, semaphores):
    return [
        pltpu.make_async_copy(source.at[:, pl.ds(at, wide)], target.at[:, pl.ds(at, wide)], semaphores.at[i])
        for i, (at, wide) in enumerate(chunks_of(source.shape[1]))
    ]


def back_kernel(count, has_ortho, _, *refs):
    left_refs, refs = refs[:count], refs[count:]
    one_ref, two_ref, refs = refs[0], refs[1], refs[2:]
    if has_ortho:
        earlier_ref, refs = refs[0], refs[1:]
    buffer_ref, ortho_ref, back_ref, held, arrived = refs
    coming = copies(buffer_ref, held, arrived)
    for copy in coming:
        copy.start()
    left = [ref[...] for ref in left_refs]
    total = lax.dot_general(
        jnp.concatenate(left + left, axis=1),
        jnp.concatenate([one_ref[...], two_ref[...]], axis=1),
        (((1,), (1,)), ((), ())),
        preferred_element_type=f32,
    )
    if has_ortho:
        ortho_ref[:, : earlier_ref.shape[1]] = earlier_ref[...]
        ortho_ref[:, earlier_ref.shape[1] :] = total.astype(bf16)
    else:
        ortho_ref[...] = total.astype(bf16)
    turned = total.T.astype(bf16)
    for copy, (at, wide) in zip(coming, chunks_of(held.shape[1])):
        copy.wait()
        back_ref[:, at : at + wide] = jnp.dot(
            turned, held[:, at : at + wide], preferred_element_type=f32
        ).astype(bf16)


def back_product(before, lefts, one, two, earlier, buffer):
    rows, columns = buffer.shape
    rank = one.shape[0]
    extra = [] if earlier is None else [earlier]
    all_rank = rank + sum(v.shape[1] for v in extra)
    return pl.pallas_call(
        functools.partial(back_kernel, len(lefts), bool(extra)),
        out_shape=[
            jax.ShapeDtypeStruct((rows, all_rank), bf16),
            jax.ShapeDtypeStruct((rank, columns), bf16),
        ],
        in_specs=[UNREAD] + [IN_VMEM] * (len(lefts) + 2 + len(extra)) + [ANYWHERE],
        out_specs=[IN_VMEM, IN_VMEM],
        scratch_shapes=[
            pltpu.VMEM((rows, columns), bf16),
            pltpu.SemaphoreType.DMA((len(chunks_of(columns)),)),
        ],
        compiler_params=BIG,
        cost_estimate=SHORT,
        name="back_product",
    )(before, *lefts, one, two, *extra, buffer)


def pick_kernel(which_ref, part_ref, _, out_ref):
    rows = out_ref.shape[0]
    out_ref[...] = part_ref[pl.ds(pl.multiple_of(which_ref[0] * rows, rows), rows), :]


def pick(part, which, earlier):
    return pl.pallas_call(
        pick_kernel,
        out_shape=jax.ShapeDtypeStruct((part.shape[0] // 2, part.shape[1]), part.dtype),
        in_specs=[pl.BlockSpec(memory_space=pltpu.SMEM), IN_VMEM, UNREAD],
        out_specs=IN_VMEM,
        compiler_params=pltpu.CompilerParams(vmem_limit_bytes=16 << 20),
        cost_estimate=SHORT,
        name="pick",
    )(which.reshape(1).astype(jnp.int32), part, earlier)


def join_kernel(first_ref, own_ref, other_ref, _, out_ref):
    rows = own_ref.shape[0]
    at = first_ref[0]
    out_ref[pl.ds(pl.multiple_of(at * rows, rows), rows), :] = own_ref[...]
    out_ref[pl.ds(pl.multiple_of((1 - at) * rows, rows), rows), :] = other_ref[...]


def join(own, other, at, earlier):
    return pl.pallas_call(
        join_kernel,
        out_shape=jax.ShapeDtypeStruct((2 * own.shape[0], own.shape[1]), own.dtype),
        in_specs=[pl.BlockSpec(memory_space=pltpu.SMEM), IN_VMEM, IN_VMEM, UNREAD],
        out_specs=IN_VMEM,
        compiler_params=pltpu.CompilerParams(vmem_limit_bytes=16 << 20),
        cost_estimate=SHORT,
        name="join",
    )(at.reshape(1).astype(jnp.int32), own, other, earlier)


def total_kernel(*refs):
    *part_refs, _, out_ref = refs
    total = part_refs[0][...]
    for ref in part_refs[1:]:
        total = total + ref[...]
    out_ref[...] = total.astype(out_ref.dtype)


def total_of(parts, dtype, earlier):
    return pl.pallas_call(
        total_kernel,
        out_shape=jax.ShapeDtypeStruct(parts[0].shape, dtype),
        in_specs=[IN_VMEM] * len(parts) + [ANYWHERE],
        out_specs=IN_VMEM,
        compiler_params=pltpu.CompilerParams(vmem_limit_bytes=8 << 20),
        cost_estimate=SHORT,
        name="total",
    )(*parts, earlier)


def finish_kernel(own_ref, other_ref, _, out_ref, square_ref):
    total = own_ref[...].astype(f32) + other_ref[...].astype(f32)
    out_ref[...] = total.astype(bf16)
    square_ref[...] = jnp.broadcast_to(jnp.sum(total * total, axis=1, keepdims=True), square_ref.shape)


def finish(own, other, earlier):
    rows = own.shape[0]
    return pl.pallas_call(
        finish_kernel,
        out_shape=[jax.ShapeDtypeStruct(own.shape, bf16), jax.ShapeDtypeStruct((rows, LANES), f32)],
        in_specs=[IN_VMEM, IN_VMEM, UNREAD],
        out_specs=[IN_VMEM, IN_VMEM],
        compiler_params=pltpu.CompilerParams(vmem_limit_bytes=16 << 20),
        cost_estimate=SHORT,
        name="finish",
    )(own, other, earlier)


def update_kernel(cut, scaled, ortho_ref, *refs):
    back_refs, refs = refs[:PIECES], refs[PIECES:]
    if scaled:
        scale_ref, refs = refs[0], refs[1:]
        upright = scale_ref[...].T
        scales = [
            jnp.concatenate([upright[:, p : p + 1], upright[:, PIECES + p : PIECES + p + 1]], axis=0)
            for p in range(PIECES)
        ]
        value_ref, out_ref, right_ref, held, arrived, left, turned, turned_left = refs
    else:
        value_ref, out_ref, token_ref, held, arrived, left = refs
        token_ref[...] = jnp.zeros_like(token_ref)
    coming = copies(value_ref, held, arrived)
    going = copies(held, out_ref, left)
    for copy in coming:
        copy.start()
    rows, columns = held.shape
    tall = min(512, rows)
    leaving = []
    for i, (at, wide) in enumerate(chunks_of(columns)):
        backs = [ref[:, at : at + wide] for ref in back_refs]
        if scaled:
            rights = [v.astype(f32) * by for v, by in zip(backs, scales)]
            column = 0
            for v in rights:
                turned[at : at + wide, column : column + v.shape[0]] = v.T
                column += v.shape[0]
            copy = pltpu.make_async_copy(
                turned.at[pl.ds(at, wide), :], right_ref.at[pl.ds(at, wide), :], turned_left.at[i]
            )
            copy.start()
            leaving.append(copy)
            backs = [v.astype(bf16) for v in rights]
        back = jnp.concatenate(backs, axis=0)
        coming[i].wait()
        for top in range(0, rows, tall):
            here = (slice(top, top + tall), slice(at, at + wide))
            change = jnp.dot(ortho_ref[top : top + tall, :], back, preferred_element_type=f32)
            held[here] = (held[here].astype(f32) - cut * change).astype(bf16)
        going[i].start()
    for copy in going + leaving:
        copy.wait()


def update(cut, ortho, backs, scales, value, name):
    rows, columns = value.shape
    scaled = bool(scales)
    rank = sum(v.shape[0] for v in backs)
    count = len(chunks_of(columns))
    out_shape = [jax.ShapeDtypeStruct(value.shape, value.dtype)]
    scratch = [
        pltpu.VMEM((rows, columns), bf16),
        pltpu.SemaphoreType.DMA((count,)),
        pltpu.SemaphoreType.DMA((count,)),
    ]
    if scaled:
        out_shape.append(jax.ShapeDtypeStruct((columns, rank), f32))
        out_specs = [ANYWHERE] * 2
        scratch += [pltpu.VMEM((columns, rank), f32), pltpu.SemaphoreType.DMA((count,))]
    else:
        out_shape.append(jax.ShapeDtypeStruct((8, LANES), f32))
        out_specs = [ANYWHERE, IN_VMEM]
    return pl.pallas_call(
        functools.partial(update_kernel, cut, scaled),
        out_shape=out_shape,
        in_specs=[IN_VMEM] * (1 + len(backs) + len(scales)) + [ANYWHERE],
        out_specs=out_specs,
        scratch_shapes=scratch,
        compiler_params=pltpu.CompilerParams(vmem_limit_bytes=36 << 20),
        cost_estimate=SHORT,
        name=name,
    )(ortho, *backs, *scales, value)


def swap(value, axis, count, bit):
    return lax.ppermute(value, axis, [(i, i ^ bit) for i in range(count)])


def take(value, part, parts):
    share = value.shape[0] // parts
    return lax.dynamic_slice_in_dim(value, part * share, share, 0)


def in_order(first, own, other):
    return jnp.concatenate([jnp.where(first, own, other), jnp.where(first, other, own)], axis=0)


def make_on_device(n_row, n_col):
    n_line = n_col // 2

    def along(value, steps):
        return lax.ppermute(
            value, "col", [(i, (i // 2 + steps) % n_line * 2 + i % 2) for i in range(n_col)]
        )

    def on_device(weight, momentum, grad, right_factor):
        full = right_factor.shape[0] * n_col
        core = lax.axis_index("row") % 2
        side = lax.axis_index("col") % 2
        place = lax.axis_index("col") // 2

        def reduce_pair(part):
            sent = take(part, 1 - side, 2).astype(bf16)
            return take(part, side, 2) + swap(sent, "col", n_col, 1).astype(f32)

        def reduce_line(part):
            total = take(part, place, n_line)
            for d in range(1, n_line):
                total = total + along(
                    take(part, (place + d) % n_line, n_line).astype(bf16), d
                ).astype(f32)
            return total.astype(bf16)

        def gather_line(share):
            rows = share.shape[0]
            joined = jnp.zeros((n_line * rows, share.shape[1]), bf16)
            joined = lax.dynamic_update_slice_in_dim(joined, share, place * rows, 0)
            for d in range(1, n_line):
                at = (place + n_line - d) % n_line * rows
                joined = lax.dynamic_update_slice_in_dim(joined, along(share, d), at, 0)
            return joined

        def gather_pair(half):
            return in_order(side == 0, half, swap(half, "col", n_col, 1))

        def sum_cores(part):
            return take(part, core, 2) + swap(take(part, 1 - core, 2), "row", n_row, 1)

        def sum_others(half):
            bit = 2
            while bit < n_row:
                half = half + swap(half, "row", n_row, bit)
                bit *= 2
            return half

        def join_cores(half):
            return in_order(core == 0, half, swap(half, "row", n_row, 1))

        def sum_core(part, sent):
            own = take(part, core, 2).astype(f32) + swap(sent, "row", n_row, 1).astype(f32)
            return own.astype(bf16)

        def sum_chips(own, earlier):
            bit = 2
            while 2 * bit < n_row:
                own = (own.astype(f32) + swap(own, "row", n_row, bit).astype(f32)).astype(bf16)
                bit *= 2
            total, squares = finish(own, swap(own, "row", n_row, bit), earlier)
            return total, squares[:, :1].reshape(1, -1)

        def sum_squares(squares, meanwhile):
            squares = squares + swap(squares, "col", n_col, 1)
            others = [along(squares, d) for d in range(1, n_line)]
            squares = total_of([squares, *others], f32, meanwhile)
            return in_order(core == 0, squares, swap(squares, "row", n_row, 1))

        buffer = (momentum.astype(f32) + grad.astype(f32)).astype(bf16)
        right_in = right_factor.astype(bf16)
        piece = right_in.shape[1] // 2
        part_1 = jnp.dot(buffer, right_in[:, :piece], preferred_element_type=f32)
        part_2 = jnp.dot(buffer, right_in[:, piece:], preferred_element_type=f32)
        over_rows = (((0,), (0,)), ((), ()))

        pair_1 = reduce_pair(part_1)
        share_1 = reduce_line(pair_1)
        pair_2 = reduce_pair(part_2)
        line_1 = gather_line(share_1)
        share_2 = reduce_line(pair_2)
        left_1 = gather_pair(line_1)
        line_2 = gather_line(share_2)
        gram_1 = join_cores(
            sum_others(
                sum_cores(lax.dot_general(left_1, left_1, over_rows, preferred_element_type=f32))
            )
        )
        inverse_1, one_1, two_1 = first_inverse(gram_1)
        left_2 = join(line_2, swap(line_2, "col", n_col, 1), side, inverse_1)
        gram_2 = sum_cores(
            jnp.concatenate(
                [
                    lax.dot_general(left_2, left_1, over_rows, preferred_element_type=f32),
                    lax.dot_general(left_2, left_2, over_rows, preferred_element_type=f32),
                ],
                axis=1,
            )
        )
        ortho_1, back_part_1 = back_product(gram_2, [left_1], one_1, two_1, None, buffer)
        gram_2 = sum_others(gram_2)
        core_1 = sum_core(back_part_1, pick(back_part_1, 1 - core, gram_2))
        chips_1, squares_1 = sum_chips(core_1, core_1)
        one_2, two_2 = second_inverse(join_cores(gram_2), inverse_1, core_1)
        ortho, back_part_2 = back_product(core_1, [left_1, left_2], one_2, two_2, ortho_1, buffer)
        core_2 = sum_core(back_part_2, pick(back_part_2, 1 - core, chips_1))
        chips_2, squares_2 = sum_chips(core_2, core_2)
        back_1 = join_cores(chips_1)
        back_2 = join_cores(chips_2)
        momentum_next, token = update(FEEDBACK_CUT, ortho, [back_1, back_2], [], buffer, "momentum_update")
        squares = jnp.concatenate([squares_1, squares_2], axis=1).reshape(2, -1)
        squares = sum_squares(squares, token)
        squares = jnp.concatenate([squares, squares], axis=0)
        scale = jnp.sqrt(f32(full)) / jnp.sqrt(squares + EPSILON_SQ)

        weight_next, right_next = update(
            STEP_SIZE, ortho, [back_1, back_2], [scale], weight, "weight_update"
        )
        return (weight_next, momentum_next, right_next)

    return on_device


def solution(mesh):
    in_specs = (P("row", "col"), P("row", "col"), P("row", "col"), P("col", None))
    out_specs = (P("row", "col"), P("row", "col"), P("col", None))
    return jax.shard_map(
        make_on_device(mesh.shape["row"], mesh.shape["col"]),
        mesh=mesh,
        in_specs=in_specs,
        out_specs=out_specs,
        check_vma=False,
    )
```
